256 devices in a mesh: section: 8 (over y, z_hi), dp: 32 (over z_lo, x, core).
Axes of the slice: x: 4, y: 4, z: 8 (z_hi: 2, z_lo: 4; z = z_hi * 4 + z_lo), core: 2. Of those that a mesh axis runs over, the one named last changes fastest.
Arguments:
- inputs: bfloat16 [4, 2048, 2048], P(None, 'dp'), may hold values from -6 to 6
- cotangent: bfloat16 [4, 2048, 2048], P(None, 'dp'), may hold values from -6 to 6
- weight: bfloat16 [8, 2048, 2048], P('section'), may hold values from -0.125 to 0.125
- factor_old: float32 [8, 2048, 2048], P('section', 'dp'), may hold values from -1.5 to 3.5, as said below
- stale_inverse: bfloat16 [8, 2048, 2048], P('section', 'dp'), may hold values from -0.5 to 0.75, as said below
Outputs:
- input_grads: bfloat16 [8, 4, 2048, 2048], P('section', None, 'dp')
- factor_new: float32 [8, 2048, 2048], P('section', 'dp')
- inverse_new: bfloat16 [8, 2048, 2048], P('section', 'dp')
The draws below stay inside these ranges and needn't reach their ends.
Inputs may be any that keep to these rules, and one draw needn't show every extreme that they name: `factor_old`: symmetric in its last two dimensions. `stale_inverse`: symmetric in its last two dimensions.
All inputs are finite; a program needn't handle non-finite values.
Results may differ from the reference program's by a relative error of at most 0.039.
Values may be sent and summed in bfloat16 or wider, within the bound.
No kernel may reach another device: no remote copies, remote signals or barrier semaphores. Data moves between devices by JAX's collectives and lax.ppermute only.
A program may use at most 128 MiB of HBM per device.

```python
import math
import jax
import jax.numpy as jnp
from jax import lax

W = 2048
TOK_MB = 64
MICRO = 4
TOKENS = 2048
N_SECTION = 8
N_DP = 32


def symmetric_part(noise, spread):
    return (noise + jnp.swapaxes(noise, 1, 2)) * (spread / math.sqrt(2.0 * W))


def pair_fields(key, curve):
    order_keys = jax.random.split(jax.random.fold_in(key, 5), N_SECTION)
    orders = jax.vmap(lambda one_key: jax.random.permutation(one_key, W))(order_keys).astype(jnp.int32)
    places = jnp.argsort(orders, axis=1).astype(jnp.int32)
    mate_places = places + 1 - 2 * (places % 2)
    partner = jnp.take_along_axis(orders, mate_places, axis=1).astype(jnp.int32)
    columns = jnp.arange(W, dtype=jnp.int32)
    lower = jnp.minimum(columns[None, :], partner).astype(jnp.int32)
    diag_key, size_key, sign_key = jax.random.split(jax.random.fold_in(key, 9), 3)
    diagonal = 1.5 * 2.0 ** jax.random.uniform(diag_key, (N_SECTION, W), jnp.float32) ** curve
    magnitude = 0.6 + 0.7 * jax.random.uniform(size_key, (N_SECTION, W), jnp.float32) ** curve
    signs = 2.0 * jax.random.randint(sign_key, (N_SECTION, W), 0, 2).astype(jnp.float32) - 1.0
    coupling = jnp.take_along_axis(magnitude * signs, lower, axis=1)
    mate_diagonal = jnp.take_along_axis(diagonal, partner, axis=1)
    pair_mask = (columns[None, None, :] == partner[:, :, None]).astype(jnp.float32)
    return (diagonal, mate_diagonal, coupling, pair_mask, partner)


def draw_factor_old(key, part):
    diagonal, mate_diagonal, coupling, pair_mask, partner = pair_fields(key, 1.0)
    key = jax.random.fold_in(key, 11)
    noise = jnp.clip(jax.random.normal(key, (N_SECTION, W, W), jnp.float32), -4.0, 4.0)
    identity = jnp.eye(W, dtype=jnp.float32)
    return symmetric_part(noise, 0.1) + identity * diagonal[:, :, None] + pair_mask * coupling[:, :, None]


def draw_stale_inverse(key, part):
    diagonal, mate_diagonal, coupling, pair_mask, partner = pair_fields(key, 1.0)
    key = jax.random.fold_in(key, 23)
    first_key, second_key = jax.random.split(key)
    noise = jnp.clip(jax.random.normal(first_key, (N_SECTION, W, W), jnp.float32), -4.0, 4.0)
    drift = 1.0 + 0.15 * jax.random.uniform(second_key, (N_SECTION, W), jnp.float32, -1.0, 1.0)
    mate_drift = jnp.take_along_axis(drift, partner, axis=1)
    own_level = (0.25 * diagonal + 1.75) * drift
    mate_level = (0.25 * mate_diagonal + 1.75) * mate_drift
    pair_level = 0.25 * coupling
    determinant = own_level * mate_level - pair_level * pair_level
    identity = jnp.eye(W, dtype=jnp.float32)
    block_inverse = identity * (mate_level / determinant)[:, :, None] - pair_mask * (pair_level / determinant)[:, :, None]
    return (symmetric_part(noise, 0.1) + block_inverse).astype(jnp.bfloat16)


def block_levels(own_key, dims, cuts, smallest, high):
    gain = 1.0
    for axis_at, parts in cuts:
        heights = jax.random.uniform(jax.random.fold_in(jax.random.fold_in(own_key, 6), axis_at), (parts,), jnp.float32, smallest / len(cuts), high / len(cuts))
        gain = gain * jnp.repeat(jnp.exp(heights), dims[axis_at] // parts).reshape((-1,) + (1,) * (len(dims) - 1 - axis_at))
    return gain


def centred(rng, shape, scale, most, cuts=(), kind=jnp.bfloat16):
    loudness = block_levels(rng, shape, cuts, -0.22, 0.18) if cuts else 1.0
    array = jax.random.normal(rng, shape, jnp.float32) * scale * loudness
    return jnp.minimum(jnp.maximum(array, -most), most).astype(kind)


def setup_inputs(seed: int = 0) -> dict:
    splits = jax.random.split(jax.random.key(seed), 6)
    inputs = centred(splits[0], (MICRO, TOKENS, W), 1.0, 6.0, ((1, 32),))
    cotangent = centred(splits[1], (MICRO, TOKENS, W), 1.0, 6.0, ((1, 32),))
    weight = centred(splits[2], (N_SECTION, W, W), W ** -0.5, 0.125, ((0, 8),))
    factor_old = draw_factor_old(jax.random.fold_in(splits[5], 71), 0)
    stale_inverse = draw_stale_inverse(jax.random.fold_in(splits[5], 71), 0)
    return dict(inputs=inputs, cotangent=cotangent, weight=weight, factor_old=factor_old, stale_inverse=stale_inverse)


BETA = 0.25
DAMPING = 1.0


def tanh_slope(preact):
    squashed = jnp.tanh(preact)
    return 1.0 - squashed * squashed


def reference(inputs, cotangent, weight, factor_old, stale_inverse):
    hidden = inputs
    stored = []
    preacts = []
    for section_no in range(N_SECTION):
        flat_rows = hidden.reshape(-1, W)
        preact = jnp.dot(flat_rows, weight[section_no], preferred_element_type=jnp.float32)
        stored.append(hidden)
        preacts.append(preact)
        hidden = (flat_rows.astype(jnp.float32) + jnp.tanh(preact)).astype(jnp.bfloat16).reshape(hidden.shape)
    grad_rows = cotangent
    grads = [None] * N_SECTION
    for section_no in range(N_SECTION - 1, -1, -1):
        flat_grad = grad_rows.reshape(-1, W).astype(jnp.float32)
        scaled = (flat_grad * tanh_slope(preacts[section_no])).astype(jnp.bfloat16)
        back = jnp.dot(scaled, weight[section_no].T, preferred_element_type=jnp.float32)
        grad_rows = (flat_grad + back).astype(jnp.bfloat16).reshape(grad_rows.shape)
        grads[section_no] = grad_rows
    identity = jnp.eye(W, dtype=jnp.float32)
    factors = []
    inverses = []
    for section_no in range(N_SECTION):
        acts = stored[section_no]

        def add_replica(replica, running):
            block_rows = lax.dynamic_slice_in_dim(acts, (replica * TOK_MB).astype(jnp.int32), TOK_MB, 1).reshape(-1, W)
            partial_value = jnp.dot(block_rows.T, block_rows, preferred_element_type=jnp.float32).astype(jnp.bfloat16)
            partial_value = lax.optimization_barrier(partial_value)
            return running + partial_value.astype(jnp.float32)

        total_sum = lax.fori_loop(jnp.int32(0), jnp.int32(N_DP), add_replica, jnp.zeros((W, W), jnp.float32))
        factor = BETA * factor_old[section_no] + ((1.0 - BETA) / (MICRO * TOKENS)) * total_sum
        damped = (factor + DAMPING * identity).astype(jnp.bfloat16)
        product = jnp.dot(damped, stale_inverse[section_no], preferred_element_type=jnp.float32).astype(jnp.bfloat16)
        correction = jnp.dot(stale_inverse[section_no], product, preferred_element_type=jnp.float32)
        refined = (2.0 * stale_inverse[section_no].astype(jnp.float32) - correction).astype(jnp.bfloat16)
        factors.append(factor)
        inverses.append(refined)
    return jnp.stack(grads), jnp.stack(factors), jnp.stack(inverses)
```

```python
import functools

import jax
import jax.numpy as jnp
from jax import lax
from jax.experimental import pallas as pl
from jax.experimental.pallas import tpu as pltpu
from jax.sharding import PartitionSpec as P

BETA = 0.25
DAMPING = 1.0

SECTIONS = 8
REPLICAS = 32
MICROS = 4
ROWS = 64
W = 2048
BLK = 256
NBLK = W // BLK
KEEP = NBLK // 2 + 1
KW = KEEP * BLK
LAST = SECTIONS - 1
TICKS = MICROS + SECTIONS - 1
SCALE = (1.0 - BETA) / (MICROS * ROWS * REPLICAS)

bf16 = jnp.bfloat16
f32 = jnp.float32

VM = pl.BlockSpec(memory_space=pltpu.VMEM)
ANY = pl.BlockSpec(memory_space=pl.ANY)

GROUP_XC = [[z * 8 + k for k in range(8)] for z in range(4)]
GROUP_Z = [[z * 8 + k for z in range(4)] for k in range(8)]


def call(kernel, out_shape, in_specs, out_specs, scratch, name, mib, flops=0, moved=0):
    return pl.pallas_call(
        kernel,
        out_shape=out_shape,
        in_specs=in_specs,
        out_specs=out_specs,
        scratch_shapes=scratch,
        compiler_params=pltpu.CompilerParams(vmem_limit_bytes=mib << 20),
        cost_estimate=pl.CostEstimate(flops=flops, bytes_accessed=moved, transcendentals=0),
        name=name,
    )


def rows_of(kind=bf16, rows=ROWS, cols=W):
    return jax.ShapeDtypeStruct((rows, cols), kind)


LAYER_COST = dict(flops=2 * ROWS * W * W, moved=W * W * 2)


def pick(index, choices, dst, sem):
    for number, src in enumerate(choices):

        @pl.when(index == number)
        def _():
            pltpu.make_async_copy(src, dst, sem).start()


def forward_layer(x_ref, w_ref, h_ref, slope_ref):
    for j in range(NBLK):
        cols = slice(j * BLK, (j + 1) * BLK)
        squashed = jnp.tanh(jnp.dot(x_ref[...], w_ref[:, cols], preferred_element_type=f32))
        h_ref[:, cols] = (x_ref[:, cols].astype(f32) + squashed).astype(bf16)
        slope_ref[:, cols] = (1.0 - squashed * squashed).astype(bf16)


def forward_tick(tick, inputs, arriving, weight):
    def kernel(inputs_ref, arriving_ref, w_ref, h_ref, slope_ref, x_scr, sem):
        section = lax.axis_index("section")
        micro = tick - section

        @pl.when((micro >= 0) & (micro < MICROS))
        def _():
            if tick < MICROS:

                @pl.when(section == 0)
                def _():
                    copy = pltpu.make_async_copy(inputs_ref.at[tick], x_scr, sem)
                    copy.start()
                    copy.wait()

            if tick > 0:

                @pl.when(section != 0)
                def _():
                    x_scr[...] = arriving_ref[...]

            forward_layer(x_scr, w_ref, h_ref, slope_ref)

    return call(
        kernel,
        [rows_of(), rows_of()],
        [ANY, VM, VM],
        [VM, VM],
        [pltpu.VMEM((ROWS, W), bf16), pltpu.SemaphoreType.DMA],
        "forward_tick",
        24,
        **LAYER_COST,
    )(inputs, arriving, weight)


def backward_tick(tick, cotangent, arriving, slopes, weight):
    def kernel(cot_ref, arriving_ref, w_ref, *rest):
        slope_refs = rest[: len(slopes)]
        g_ref, u_scr, slope_scr, scaled, sem, sem_slope = rest[len(slopes) :]
        section = lax.axis_index("section")
        micro = tick - (LAST - section)

        @pl.when((micro >= 0) & (micro < MICROS))
        def _():
            pick(section + micro, slope_refs, slope_scr, sem_slope)
            if tick < MICROS:

                @pl.when(section == LAST)
                def _():
                    copy = pltpu.make_async_copy(cot_ref.at[tick], u_scr, sem)
                    copy.start()
                    copy.wait()

            if tick > 0:

                @pl.when(section != LAST)
                def _():
                    u_scr[...] = arriving_ref[...]

            pltpu.make_async_copy(slope_refs[0], slope_scr, sem_slope).wait()
            scaled[...] = (u_scr[...].astype(f32) * slope_scr[...].astype(f32)).astype(bf16)
            for j in range(NBLK):
                cols = slice(j * BLK, (j + 1) * BLK)
                back = lax.dot_general(
                    scaled[...], w_ref[cols, :], (((1,), (1,)), ((), ())), preferred_element_type=f32
                )
                g_ref[:, cols] = (u_scr[:, cols].astype(f32) + back).astype(bf16)

    return call(
        kernel,
        rows_of(),
        [ANY, VM, VM] + [ANY] * len(slopes),
        VM,
        [pltpu.VMEM((ROWS, W), bf16)] * 3 + [pltpu.SemaphoreType.DMA] * 2,
        "backward_tick",
        24,
        **LAYER_COST,
    )(cotangent, arriving, weight, *slopes)


def gram(inputs, arrivals):
    def kernel(inputs_ref, *rest):
        arrival_refs = rest[: len(arrivals)]
        out_ref, hid, obuf, sems, osems = rest[len(arrivals) :]
        section = lax.axis_index("section")

        def slot(m):
            return hid.at[pl.ds(m * ROWS, ROWS), pl.ds(0, W)]

        for m in range(MICROS):

            @pl.when(section == 0)
            def _():
                pltpu.make_async_copy(inputs_ref.at[m], slot(m), sems.at[m]).start()

            pick(section + m - 1 + 100 * (section == 0).astype(jnp.int32), arrival_refs, slot(m), sems.at[m])
        for m in range(MICROS):
            pltpu.make_async_copy(inputs_ref.at[m], slot(m), sems.at[m]).wait()
        hid[:, W:] = hid[:, : KW - BLK]
        writes = []
        for i in range(NBLK):
            left = hid[:, i * BLK : (i + 1) * BLK]
            part = lax.dot_general(
                left, hid[:, i * BLK : i * BLK + KW], (((0,), (0,)), ((), ())), preferred_element_type=f32
            ).astype(bf16)
            for k in range(BLK // ROWS):
                device = i * (BLK // ROWS) + k
                at = (device % 8) * 4 + device // 8
                obuf[at * ROWS : (at + 1) * ROWS, :] = part[k * ROWS : (k + 1) * ROWS]
                span = pl.ds(at * ROWS, ROWS)
                copy = pltpu.make_async_copy(obuf.at[span], out_ref.at[span], osems.at[at])
                copy.start()
                writes.append(copy)
        for copy in writes:
            copy.wait()

    return call(
        kernel,
        rows_of(rows=W, cols=KW),
        [ANY] * (1 + len(arrivals)),
        ANY,
        [
            pltpu.VMEM((MICROS * ROWS, W + KW - BLK), bf16),
            pltpu.VMEM((W, KW), bf16),
            pltpu.SemaphoreType.DMA((MICROS,)),
            pltpu.SemaphoreType.DMA((REPLICAS,)),
        ],
        "gram",
        32,
        flops=2 * MICROS * ROWS * W * KW,
        moved=W * KW * 2,
    )(inputs, *arrivals)


def own_block():
    replica = lax.axis_index("dp")
    per_block = BLK // ROWS
    return replica // per_block, lax.rem(replica, per_block)


def block_cols(number):
    return pl.ds(pl.multiple_of(number * BLK, BLK), BLK)


def kept_columns(stale_rows):
    def kernel(s_ref, out_ref):
        block, part = own_block()
        for k in range(KEEP):
            out_ref[:, k * BLK : (k + 1) * BLK] = s_ref[:, block_cols(lax.rem(block + k, NBLK))]

    return call(kernel, rows_of(cols=KW), [VM], VM, [], "kept_columns", 8)(stale_rows)


def damped_rows(gram_rows, factor_old):
    def kernel(g_ref, f_ref, out_ref):
        block, part = own_block()
        for k in range(KEEP):
            cols = slice(k * BLK, (k + 1) * BLK)
            old = f_ref[:, block_cols(lax.rem(block + k, NBLK))]
            value = BETA * old + SCALE * g_ref[:, cols].astype(f32)
            if k == 0:
                column = lax.broadcasted_iota(jnp.int32, (ROWS, BLK), 1)
                row = lax.broadcasted_iota(jnp.int32, (ROWS, BLK), 0) + part * ROWS
                value = value + DAMPING * (column == row).astype(f32)
            out_ref[:, cols] = value.astype(bf16)

    return call(kernel, rows_of(cols=KW), [VM, VM], VM, [], "damped_rows", 8)(gram_rows, factor_old)


def times_symmetric(left_ref, mat_ref, j):
    total = None
    for i in range(NBLK):
        left = left_ref[:, i * BLK : (i + 1) * BLK]
        k = (j - i) % NBLK
        if k < KEEP:
            block = mat_ref[i * BLK : (i + 1) * BLK, k * BLK : (k + 1) * BLK]
            part = jnp.dot(left, block, preferred_element_type=f32)
        else:
            k = (i - j) % NBLK
            block = mat_ref[j * BLK : (j + 1) * BLK, k * BLK : (k + 1) * BLK]
            part = lax.dot_general(left, block, (((1,), (1,)), ((), ())), preferred_element_type=f32)
        total = part if total is None else total + part
    return total


def refresh(damped_all, stale_all, stale_rows, gram_rows, factor_old):
    def kernel(d_ref, sa_ref, s_ref, g_ref, f_ref, factor_ref, inv_ref, mid, turn):
        block, part = own_block()
        for j in range(NBLK):
            mid[:, j * BLK : (j + 1) * BLK] = times_symmetric(s_ref, d_ref, j).astype(bf16)
        for j in range(NBLK):
            cols = slice(j * BLK, (j + 1) * BLK)
            inv_ref[:, cols] = (2.0 * s_ref[:, cols].astype(f32) - times_symmetric(mid, sa_ref, j)).astype(bf16)
        for k in range(KEEP):
            cols = block_cols(lax.rem(block + k, NBLK))
            factor_ref[:, cols] = BETA * f_ref[:, cols] + SCALE * g_ref[:, k * BLK : (k + 1) * BLK].astype(f32)
        for k in range(1, NBLK - KEEP + 1):
            other = lax.rem(block + NBLK - k, NBLK)
            lanes = pl.ds(pl.multiple_of(k * BLK + (part // 2) * 128, 128), 128)
            slab = d_ref[block_cols(other), lanes]
            turn[...] = slab.astype(f32).T
            start = pl.multiple_of(lax.rem(part, 2) * ROWS, ROWS)
            factor_ref[:, block_cols(other)] = turn[pl.ds(start, ROWS), :]

    return call(
        kernel,
        [rows_of(f32), rows_of()],
        [VM] * 5,
        [VM] * 2,
        [pltpu.VMEM((ROWS, W), bf16), pltpu.VMEM((128, BLK), f32)],
        "refresh",
        32,
        flops=4 * ROWS * W * W,
        moved=4 * W * KW,
    )(damped_all, stale_all, stale_rows, gram_rows, factor_old)


def collect(leaving):
    def kernel(*refs):
        sources, (out_ref, sems) = refs[: len(leaving)], refs[len(leaving) :]
        section = lax.axis_index("section")
        for m in range(MICROS):
            pick(LAST - section + m, sources, out_ref.at[m], sems.at[m])
        for m in range(MICROS):
            pltpu.make_async_copy(sources[0], out_ref.at[m], sems.at[m]).wait()

    return call(
        kernel,
        jax.ShapeDtypeStruct((MICROS, ROWS, W), bf16),
        [ANY] * len(leaving),
        ANY,
        [pltpu.SemaphoreType.DMA((MICROS,))],
        "collect",
        8,
    )(*leaving)


def per_device(inputs, cotangent, weight, factor_old, stale_inverse):
    weight_mat = weight[0]
    factor_old = factor_old[0]
    stale_rows = stale_inverse[0]

    stale_all = lax.all_gather(kept_columns(stale_rows), "dp", axis=0, tiled=True)

    arriving = inputs[0]
    arrivals, slopes = [], []
    for tick in range(TICKS):
        leaving, slope = forward_tick(tick, inputs, arriving, weight_mat)
        slopes.append(slope)
        route = [(s, s + 1) for s in range(LAST) if 0 <= tick - s < MICROS]
        if tick < TICKS - 1:
            arriving = lax.ppermute(leaving, "section", route)
            arrivals.append(arriving)

    partial_gram = gram(inputs, arrivals)
    gram_xc = lax.psum_scatter(
        partial_gram, "dp", scatter_dimension=0, tiled=True, axis_index_groups=GROUP_XC
    )
    gram_rows = lax.psum_scatter(gram_xc, "dp", scatter_dimension=0, tiled=True, axis_index_groups=GROUP_Z)
    damped = damped_rows(gram_rows, factor_old)
    damped_all = lax.all_gather(damped, "dp", axis=0, tiled=True)
    factor, refined = refresh(damped_all, stale_all, stale_rows, gram_rows, factor_old)

    arriving = cotangent[0]
    leavings = []
    for tick in range(TICKS):
        leaving = backward_tick(tick, cotangent, arriving, slopes, weight_mat)
        leavings.append(leaving)
        route = [(s, s - 1) for s in range(1, SECTIONS) if 0 <= tick - (LAST - s) < MICROS]
        if tick < TICKS - 1:
            arriving = lax.ppermute(leaving, "section", route)
    grads = collect(leavings)
    return (grads[None], factor[None], refined[None])


def solution(mesh):
    placed = (
        P(None, "dp", None),
        P(None, "dp", None),
        P("section", None, None),
        P("section", "dp", None),
        P("section", "dp", None),
    )
    return jax.shard_map(
        per_device,
        mesh=mesh,
        in_specs=placed,
        out_specs=(
            P("section", None, "dp", None),
            P("section", "dp", None),
            P("section", "dp", None),
        ),
        check_vma=False,
    )
```

```python
import functools

import jax
import jax.numpy as jnp
from jax import lax
from jax.experimental import pallas as pl
from jax.experimental.pallas import tpu as pltpu
from jax.sharding import PartitionSpec as P

BETA = 0.25
DAMPING = 1.0

SECTIONS = 8
STAGES = SECTIONS // 2
REPLICAS = 32
MICROS = 4
ROWS = 64
W = 2048
BLK = 256
NBLK = W // BLK
KEEP = NBLK // 2 + 1
KW = KEEP * BLK
HALF = KW // 2
CHIP = 2 * ROWS
RING = 4
TICKS = STAGES + 1
SCALE = (1.0 - BETA) / (MICROS * ROWS * REPLICAS)

bf16 = jnp.bfloat16
f32 = jnp.float32

VM = pl.BlockSpec(memory_space=pltpu.VMEM)
ANY = pl.BlockSpec(memory_space=pl.ANY)
DMA = pltpu.SemaphoreType.DMA


SIDE = [micro % 2 for micro in range(MICROS)]
ORDER = [[m for m in range(MICROS) if SIDE[m] == side] for side in range(2)]


def at_work(tick, stage_of):
    found = {s: tick - stage_of(s // 2) for s in range(SECTIONS)}
    return {s: number for s, number in found.items() if 0 <= number < 2}


def home_source(section, micro):
    stage, side = section // 2, section % 2
    tick = stage + ORDER[SIDE[micro]].index(micro)
    if SIDE[micro] != side:
        return ("ex", tick)
    if side == 1:
        return ("mid", tick)
    return ("arr", tick) if stage else ("in", micro)


def call(kernel, out_shape, in_specs, out_specs, scratch, name, mib, flops=0, moved=0, after=0):
    def whole(*refs):
        kernel(*refs[: len(in_specs)], *refs[len(in_specs) + after :])

    return pl.pallas_call(
        whole,
        out_shape=out_shape,
        in_specs=in_specs + [ANY] * after,
        out_specs=out_specs,
        scratch_shapes=scratch,
        compiler_params=pltpu.CompilerParams(vmem_limit_bytes=mib << 20),
        cost_estimate=pl.CostEstimate(flops=flops, bytes_accessed=moved, transcendentals=0),
        name=name,
    )


def rows_of(rows=ROWS, cols=W, kind=bf16):
    return jax.ShapeDtypeStruct((rows, cols), kind)


LAYER_COST = dict(flops=2 * ROWS * W * W, moved=W * W * 2)
PAIR_COST = dict(flops=4 * ROWS * W * W, moved=W * W * 4)


def is_any(value, numbers):
    return functools.reduce(jnp.logical_or, [value == number for number in numbers])


def pick(section, wanted, choices, dst, sem):
    for tag, src in choices.items():
        users = [number for number, name in wanted.items() if name == tag]
        if users:

            @pl.when(is_any(section, users))
            def _():
                pltpu.make_async_copy(src, dst, sem).start()


def place():
    replica = lax.axis_index("dp")
    return replica // 8, lax.rem(replica // 2, RING), lax.rem(replica, 2)


def each_block(body):
    @pl.loop(0, NBLK // 4)
    def _(group):
        for k in range(4):
            body(pl.ds(pl.multiple_of((group * 4 + k) * BLK, BLK), BLK))


def forward_layer(x_ref, w_ref, h_ref, slope_ref):
    def body(cols):
        squashed = jnp.tanh(jnp.dot(x_ref[...], w_ref[:, cols], preferred_element_type=f32))
        h_ref[:, cols] = (x_ref[:, cols].astype(f32) + squashed).astype(bf16)
        slope_ref[:, cols] = (1.0 - squashed * squashed).astype(bf16)

    each_block(body)


def resident(array, after):
    def kernel(array_ref, out_ref, sem):
        copy = pltpu.make_async_copy(array_ref, out_ref, sem)
        copy.start()
        copy.wait()

    out = pltpu.VMEM(array.shape, array.dtype)
    return call(kernel, out, [ANY], VM, [DMA], "resident", 4, after=len(after))(in_hbm(array), *after)


def both_weights(own, other):
    def kernel(own_ref, other_ref, out_ref, sems):
        side = lax.rem(lax.axis_index("section"), 2)
        copies = [
            pltpu.make_async_copy(own_ref, out_ref.at[side], sems.at[0]),
            pltpu.make_async_copy(other_ref, out_ref.at[1 - side], sems.at[1]),
        ]
        for copy in copies:
            copy.start()
        for copy in copies:
            copy.wait()

    return call(
        kernel, pltpu.VMEM((2, W, W), bf16), [ANY] * 2, VM, [DMA((2,))], "both_weights", 4
    )(in_hbm(own), in_hbm(other))


def in_vmem(array):
    return pltpu.with_memory_space_constraint(array, pltpu.VMEM)


def in_hbm(array):
    return pltpu.with_memory_space_constraint(array, pltpu.HBM)


def forward_pair(tick, inputs, arriving, weights, after):
    working = at_work(tick, lambda stage: stage)
    first = {s: ORDER[s % 2][number] for s, number in working.items() if s < 2}

    def kernel(inputs_ref, arriving_ref, w_ref, *rest):
        h_ref, mid_ref, send_ref, even_ref, odd_ref, x_scr, sem = rest
        section = lax.axis_index("section")
        side = lax.rem(section, 2)

        @pl.when(is_any(section, working))
        def _():
            if first:

                @pl.when(is_any(section, first))
                def _():
                    pick(section, first, {m: inputs_ref.at[m] for m in range(MICROS)}, x_scr, sem)
                    pltpu.make_async_copy(inputs_ref.at[0], x_scr, sem).wait()

            if len(first) < len(working):

                @pl.when(section > 1)
                def _():
                    x_scr[...] = arriving_ref[...]

            forward_layer(x_scr, w_ref.at[0], mid_ref, even_ref)
            forward_layer(mid_ref, w_ref.at[1], h_ref, odd_ref)

            @pl.when(side == 0)
            def _():
                send_ref[...] = mid_ref[...]

            @pl.when(side == 1)
            def _():
                send_ref[...] = x_scr[...]

    return call(
        kernel,
        [rows_of()] * 5,
        [ANY, VM, VM],
        [VM] * 5,
        [pltpu.VMEM((ROWS, W), bf16), DMA],
        "forward_pair",
        12,
        after=len(after),
        **PAIR_COST,
    )(inputs, arriving, in_vmem(weights), *after)


def backward_layer(u_ref, slope_ref, w_ref, scaled, g_ref):
    scaled[...] = (u_ref[...].astype(f32) * slope_ref[...].astype(f32)).astype(bf16)

    def body(cols):
        back = lax.dot_general(
            scaled[...], w_ref[cols, :], (((1,), (1,)), ((), ())), preferred_element_type=f32
        )
        g_ref[:, cols] = (u_ref[:, cols].astype(f32) + back).astype(bf16)

    each_block(body)


def backward_pair(tick, cotangent, arriving, slopes, weights, after):
    working = at_work(tick, lambda stage: STAGES - 1 - stage)
    even_tags = {s: ("even", s // 2 + number) for s, number in working.items()}
    odd_tags = {s: ("odd", s // 2 + number) for s, number in working.items()}
    first = {s: ORDER[s % 2][number] for s, number in working.items() if s // 2 == STAGES - 1}
    names = sorted({*even_tags.values(), *odd_tags.values()})
    count = len(names)

    def kernel(cot_ref, arriving_ref, w_ref, *rest):
        choices = dict(zip(names, rest[:count]))
        low_ref, keep_ref, send_ref, u_scr, even_scr, odd_scr, scaled, sems = rest[count:]
        section = lax.axis_index("section")
        side = lax.rem(section, 2)

        @pl.when(is_any(section, working))
        def _():
            pick(section, odd_tags, choices, odd_scr, sems.at[0])
            pick(section, even_tags, choices, even_scr, sems.at[1])

            if first:
                pick(section, first, {m: cot_ref.at[m] for m in range(MICROS)}, u_scr, sems.at[2])

                @pl.when(is_any(section, first))
                def _():
                    pltpu.make_async_copy(cot_ref.at[0], u_scr, sems.at[2]).wait()

            if len(first) < len(working):

                @pl.when(jnp.logical_not(is_any(section, list(first) or [-1])))
                def _():
                    u_scr[...] = arriving_ref[...]

            pltpu.make_async_copy(rest[0], odd_scr, sems.at[0]).wait()
            pltpu.make_async_copy(rest[0], even_scr, sems.at[1]).wait()

            backward_layer(u_scr, odd_scr, w_ref.at[1], scaled, keep_ref)
            backward_layer(keep_ref, even_scr, w_ref.at[0], scaled, low_ref)

            @pl.when(side == 0)
            def _():
                send_ref[...] = keep_ref[...]
                keep_ref[...] = low_ref[...]

            @pl.when(side == 1)
            def _():
                send_ref[...] = low_ref[...]

    return call(
        kernel,
        [rows_of()] * 3,
        [ANY, VM, VM] + [ANY] * count,
        [VM] * 3,
        [pltpu.VMEM((ROWS, W), bf16)] * 4 + [DMA((3,))],
        "backward_pair",
        12,
        after=len(after),
        **PAIR_COST,
    )(cotangent, arriving, in_vmem(weights), *[slopes[name] for name in names], *after)


def collect(keeps, received, after):
    ticks = len(keeps)

    def kernel(*refs):
        choices = {("keep", b): refs[b] for b in range(ticks)}
        choices.update({("got", b): refs[ticks + b] for b in range(ticks)})
        out_ref, sems = refs[2 * ticks :]
        section = lax.axis_index("section")
        for m in range(MICROS):
            wanted = {}
            for s in range(SECTIONS):
                b = STAGES - 1 - s // 2 + ORDER[SIDE[m]].index(m)
                wanted[s] = ("keep" if SIDE[m] == s % 2 else "got", b)
            pick(section, wanted, choices, out_ref.at[m], sems.at[m])
        for m in range(MICROS):
            pltpu.make_async_copy(refs[0], out_ref.at[m], sems.at[m]).wait()

    return call(
        kernel,
        jax.ShapeDtypeStruct((MICROS, ROWS, W), bf16),
        [ANY] * (2 * ticks),
        ANY,
        [DMA((MICROS,))],
        "collect",
        8,
        after=len(after),
    )(*keeps, *received, *after)


def pack_home(inputs, held, after):
    names = list(held)

    def kernel(inputs_ref, *rest):
        choices = dict(zip(names, rest))
        choices.update({("in", m): inputs_ref.at[m] for m in range(MICROS)})
        out_ref, sems = rest[len(names) :]
        section = lax.axis_index("section")

        def slot(m):
            return out_ref.at[pl.ds(m * ROWS, ROWS)]

        for m in range(MICROS):
            pick(section, {s: home_source(s, m) for s in range(SECTIONS)}, choices, slot(m), sems.at[m])
        for m in range(MICROS):
            pltpu.make_async_copy(inputs_ref.at[m], slot(m), sems.at[m]).wait()

    return call(
        kernel,
        rows_of(MICROS * ROWS),
        [ANY] * (1 + len(names)),
        VM,
        [DMA((MICROS,))],
        "pack_home",
        8,
        after=len(after),
    )(inputs, *held.values(), *after)


def gram(own, mate):
    def kernel(own_ref, mate_ref, far_up, far_down, up, down, here, hid):
        z, x, core = place()
        tokens = MICROS * ROWS
        for number, ref in enumerate((own_ref, mate_ref)):
            span = slice(number * tokens, (number + 1) * tokens)
            hid[span, :W] = ref[...]
            hid[span, W:] = ref[:, : KW - BLK]
        jobs = [(far_up, 2, 0, 0), (far_up, 2, 1, 1), (far_down, 2, 2, 0), (far_down, 2, 3, 1)]
        jobs += [(ref, ahead, k, k) for ref, ahead in ((up, 1), (down, 3), (here, 0)) for k in range(RING)]
        for out_ref, ahead, chunk, row in jobs:
            column = lax.rem(x + ahead, RING)
            left = pl.ds(pl.multiple_of(chunk * RING * CHIP + column * CHIP, CHIP), CHIP)
            block = chunk * 2 + column // 2
            right = pl.ds(pl.multiple_of(block * BLK + core * HALF, 128), HALF)
            part = lax.dot_general(
                hid[:, left], hid[:, right], (((0,), (0,)), ((), ())), preferred_element_type=f32
            )
            out_ref[row * CHIP : (row + 1) * CHIP, :] = part.astype(bf16)

    return call(
        kernel,
        [rows_of(2 * CHIP, HALF)] * 2 + [rows_of(RING * CHIP, HALF)] * 3,
        [VM] * 2,
        [VM] * 5,
        [pltpu.VMEM((2 * MICROS * ROWS, W + KW - BLK), bf16)],
        "gram",
        32,
        flops=4 * MICROS * ROWS * W * HALF,
        moved=W * KW,
    )(own, mate)


def add_far(up, down, got_up, got_down, after):
    def kernel(up_ref, down_ref, gu_ref, gd_ref, new_up, new_down):
        near, far = slice(0, 2 * CHIP), slice(2 * CHIP, 4 * CHIP)
        new_up[near] = (up_ref[near].astype(f32) + gu_ref[...].astype(f32)).astype(bf16)
        new_up[far] = up_ref[far]
        new_down[near] = down_ref[near]
        new_down[far] = (down_ref[far].astype(f32) + gd_ref[...].astype(f32)).astype(bf16)

    return call(
        kernel,
        [rows_of(RING * CHIP, HALF)] * 2,
        [VM] * 4,
        [VM] * 2,
        [],
        "add_far",
        16,
        after=len(after),
    )(up, down, got_up, got_down, *after)


def add_near(here, got_up, got_down, after):
    def kernel(here_ref, gu_ref, gd_ref, own, one, two, three):
        z, x, core = place()
        for out_ref, mate in zip((own, one, two, three), (z, z ^ 1, z ^ 2, z ^ 3)):
            span = pl.ds(pl.multiple_of(mate * CHIP, CHIP), CHIP)
            total = here_ref[span].astype(f32) + gu_ref[span].astype(f32) + gd_ref[span].astype(f32)
            out_ref[...] = total.astype(out_ref.dtype)

    return call(
        kernel,
        [rows_of(CHIP, HALF, f32)] + [rows_of(CHIP, HALF)] * 3,
        [VM] * 3,
        [VM] * 4,
        [],
        "add_near",
        16,
        after=len(after),
    )(here, got_up, got_down, *after)


def damp(own, got, factor_old, factor_mate, after):
    def kernel(own_ref, g1, g2, g3, f_ref, fm_ref, damped_ref, sum_ref, old):
        z, x, core = place()
        block = z * 2 + x // 2
        pieces = HALF // 128
        for number in range(pieces):
            first = lax.rem(block * 2 + core * pieces + number, W // 128)
            cols = pl.ds(pl.multiple_of(first * 128, 128), 128)
            to = slice(number * 128, (number + 1) * 128)
            old[pl.ds(pl.multiple_of(core * ROWS, ROWS), ROWS), to] = f_ref[:, cols]
            old[pl.ds(pl.multiple_of((1 - core) * ROWS, ROWS), ROWS), to] = fm_ref[:, cols]
        total = own_ref[...] + g1[...].astype(f32) + g2[...].astype(f32) + g3[...].astype(f32)
        sum_ref[...] = total.astype(bf16)
        row = lax.broadcasted_iota(jnp.int32, (CHIP, HALF), 0) + lax.rem(x, 2) * CHIP
        column = lax.broadcasted_iota(jnp.int32, (CHIP, HALF), 1) + core * HALF
        diagonal = DAMPING * (row == column).astype(f32)
        damped_ref[...] = (BETA * old[...] + SCALE * total + diagonal).astype(bf16)

    return call(
        kernel,
        [rows_of(CHIP, HALF)] * 2,
        [VM] * 6,
        [VM] * 2,
        [pltpu.VMEM((CHIP, HALF), f32)],
        "damp",
        16,
        after=len(after),
    )(own, *got, factor_old, factor_mate, *after)


def stack_chunks(own, got, after):
    def kernel(own_ref, g1, g2, g3, out_ref):
        z, x, core = place()
        for ref, mate in zip((own_ref, g1, g2, g3), (z, z ^ 1, z ^ 2, z ^ 3)):
            out_ref[pl.ds(pl.multiple_of(mate * CHIP, CHIP), CHIP)] = ref[...]

    return call(
        kernel, rows_of(RING * CHIP, HALF), [VM] * 4, VM, [], "stack_chunks", 16, after=len(after)
    )(own, *got, *after)


def block_cols(number):
    return pl.ds(pl.multiple_of(number * BLK, BLK), BLK)


def kept_columns(stale_rows, after):
    def kernel(s_ref, out_ref):
        block = lax.axis_index("dp") // (BLK // ROWS)
        for k in range(KEEP):
            out_ref[:, k * BLK : (k + 1) * BLK] = s_ref[:, block_cols(lax.rem(block + k, NBLK))]

    return call(
        kernel, rows_of(cols=KW), [VM], VM, [], "kept_columns", 8, after=len(after)
    )(stale_rows, *after)


def times_symmetric(left_ref, mat_ref, j):
    total = None
    for i in range(NBLK):
        left = left_ref[:, i * BLK : (i + 1) * BLK]
        k = (j - i) % NBLK
        if k < KEEP:
            block = mat_ref[i * BLK : (i + 1) * BLK, k * BLK : (k + 1) * BLK]
            part = jnp.dot(left, block, preferred_element_type=f32)
        else:
            k = (i - j) % NBLK
            block = mat_ref[j * BLK : (j + 1) * BLK, k * BLK : (k + 1) * BLK]
            part = lax.dot_general(left, block, (((1,), (1,)), ((), ())), preferred_element_type=f32)
        total = part if total is None else total + part
    return total


def refresh(pieces, mate_pieces, stale_all, stale_rows, sums, mate_sums, factor_old, after):
    def kernel(sa_ref, s_ref, g_ref, gm_ref, f_ref, *rest):
        count = len(pieces)
        refs = rest[: 2 * count]
        factor_ref, inv_ref, damped, mid, turn, sums_scr, sems = rest[2 * count :]
        z, x, core = place()
        copies = []
        for whose in range(2):
            side = core if whose == 0 else 1 - core
            cols = pl.ds(pl.multiple_of(side * HALF, 128), HALF)
            for number, (_, ahead, first, chunks) in enumerate(pieces):
                ref = refs[whose * count + number]
                column = lax.rem(x + ahead, RING)
                for k in range(chunks):
                    start = (first + k) * RING * CHIP + column * CHIP
                    to = damped.at[pl.ds(pl.multiple_of(start, CHIP), CHIP), cols]
                    source = ref.at[pl.ds(k * CHIP, CHIP)]
                    copy = pltpu.make_async_copy(source, to, sems.at[len(copies)])
                    copy.start()
                    copies.append(copy)
        sums_scr[:, pl.ds(pl.multiple_of(core * HALF, 128), HALF)] = g_ref[...].astype(f32)
        sums_scr[:, pl.ds(pl.multiple_of((1 - core) * HALF, 128), HALF)] = gm_ref[...].astype(f32)
        block = z * 2 + x // 2
        own = pl.ds(pl.multiple_of(core * ROWS, ROWS), ROWS)
        for k in range(KEEP):
            cols = block_cols(lax.rem(block + k, NBLK))
            factor_ref[:, cols] = BETA * f_ref[:, cols] + SCALE * sums_scr[own, k * BLK : (k + 1) * BLK]
        for copy in copies:
            copy.wait()
        for j in range(NBLK):
            mid[:, j * BLK : (j + 1) * BLK] = times_symmetric(s_ref, damped, j).astype(bf16)
        for j in range(NBLK):
            cols = slice(j * BLK, (j + 1) * BLK)
            inv_ref[:, cols] = (2.0 * s_ref[:, cols].astype(f32) - times_symmetric(mid, sa_ref, j)).astype(bf16)
        for k in range(1, NBLK - KEEP + 1):
            other = lax.rem(block + NBLK - k, NBLK)
            lanes = pl.ds(pl.multiple_of(k * BLK + lax.rem(x, 2) * CHIP, CHIP), CHIP)
            turn[...] = damped[block_cols(other), lanes].astype(f32).T
            factor_ref[:, block_cols(other)] = turn[own, :]

    arrays = [piece[0] for piece in pieces]
    total = 2 * sum(piece[3] for piece in pieces)
    return call(
        kernel,
        [rows_of(kind=f32), rows_of()],
        [VM] * 5 + [ANY] * (2 * len(pieces)),
        [VM] * 2,
        [
            pltpu.VMEM((W, KW), bf16),
            pltpu.VMEM((ROWS, W), bf16),
            pltpu.VMEM((CHIP, BLK), f32),
            pltpu.VMEM((CHIP, KW), f32),
            DMA((total,)),
        ],
        "refresh",
        24,
        flops=4 * ROWS * W * W,
        moved=4 * W * KW,
        after=len(after),
    )(in_vmem(stale_all), in_hbm(stale_rows), sums, mate_sums, in_hbm(factor_old), *arrays, *mate_pieces, *after)


def hop(block, pairs):
    return lax.ppermute(block, "section", pairs)


def to_core(block):
    return lax.ppermute(block, "dp", [(r, r ^ 1) for r in range(REPLICAS)])


def along_x(block, step):
    return lax.ppermute(block, "dp", [(r, r // 8 * 8 + (r + 2 * step) % 8) for r in range(REPLICAS)])


def across_z(block, bits):
    return lax.ppermute(block, "dp", [(r, r ^ (8 * bits)) for r in range(REPLICAS)])


def per_device(inputs, cotangent, weight, factor_old, stale_inverse):
    factor_old = factor_old[0]
    stale_rows = stale_inverse[0]

    share = lax.dynamic_slice_in_dim(weight[0], lax.axis_index("dp") * ROWS, ROWS, 0)
    share = hop(share, [(s, s ^ 1) for s in range(SECTIONS)])
    weights = both_weights(weight[0], lax.all_gather(share, "dp", axis=0, tiled=True))
    stale_all = lax.all_gather(kept_columns(stale_rows, [share]), "dp", axis=0, tiled=True)
    factor_mate = to_core(factor_old)

    arriving = inputs[0]
    held, slopes = {}, {}
    for tick in range(TICKS):
        leaving, held["mid", tick], sending, slopes["even", tick], slopes["odd", tick] = forward_pair(
            tick, inputs, arriving, weights, [held["ex", tick - 2]] if tick >= 2 else []
        )
        working = at_work(tick, lambda stage: stage)
        held["ex", tick] = hop(sending, [(s, s ^ 1) for s in working])
        if tick < TICKS - 1:
            arriving = held["arr", tick + 1] = hop(leaving, [(s, s + 2) for s in working if s // 2 < STAGES - 1])

    state = dict(arriving=cotangent[0])
    keeps, received = [], []

    def backward(tick, *after):
        low, keep, send = backward_pair(
            tick, cotangent, state["arriving"], slopes, weights, after
        )
        working = at_work(tick, lambda stage: STAGES - 1 - stage)
        route = [(s, s - 2) for s in working if s >= 2]
        if tick < STAGES:
            state["arriving"] = hop(low, route)
        received.append(hop(send, [(s, s ^ 1) for s in working]))
        keeps.append(keep)
        return state["arriving"] if tick < STAGES else keep

    backward(0)
    done = backward(1)
    hidden = pack_home(inputs, held, [done])
    far_up, far_down, up, down, here = gram(hidden, to_core(hidden))
    got_up, got_down = along_x(far_up, 1), along_x(far_down, -1)
    done = backward(2, here)
    up, down = add_far(up, down, got_up, got_down, [done, received[0], received[1]])
    got_up, got_down = along_x(up, 1), along_x(down, -1)
    done = backward(3, up)
    chunk, *sending = add_near(here, got_up, got_down, [done, received[2]])
    got = [across_z(block, bits + 1) for bits, block in enumerate(sending)]
    done = backward(4, chunk)
    damped, sums = damp(chunk, got, factor_old, factor_mate, [done, received[3]])
    got = [across_z(damped, bits) for bits in (1, 2, 3)]
    mate_sums = to_core(sums)
    stale_all = resident(stale_all, [damped])
    mine = stack_chunks(damped, got, [stale_all])
    before, behind = along_x(mine, 1), along_x(mine, -1)
    far_low = along_x(before[: 2 * CHIP], 1)
    far_high = along_x(behind[2 * CHIP :], -1)
    pieces = [(mine, 0, 0, 4), (before, 3, 0, 4), (behind, 1, 0, 4), (far_low, 2, 0, 2), (far_high, 2, 2, 2)]
    mate_pieces = [to_core(piece[0]) for piece in pieces]
    grads = collect(keeps, received, [mine])
    factor, refined = refresh(
        pieces, mate_pieces, stale_all, stale_rows, sums, mate_sums, factor_old, [grads]
    )
    return (grads[None], factor[None], refined[None])


def solution(mesh):
    placed = (
        P(None, "dp", None),
        P(None, "dp", None),
        P("section", None, None),
        P("section", "dp", None),
        P("section", "dp", None),
    )
    return jax.shard_map(
        per_device,
        mesh=mesh,
        in_specs=placed,
        out_specs=(
            P("section", None, "dp", None),
            P("section", "dp", None),
            P("section", "dp", None),
        ),
        check_vma=False,
    )
```

```python
import functools

import jax
import jax.numpy as jnp
from jax import lax
from jax.experimental import pallas as pl
from jax.experimental.pallas import tpu as pltpu
from jax.sharding import PartitionSpec as P

BETA = 0.25
DAMPING = 1.0

SECTIONS = 8
STAGES = SECTIONS // 2
REPLICAS = 32
MICROS = 4
ROWS = 64
W = 2048
BLK = 256
NBLK = W // BLK
KEEP = NBLK // 2 + 1
KW = KEEP * BLK
HALF = KW // 2
CHIP = 2 * ROWS
RING = 4
TICKS = STAGES + 1
SCALE = (1.0 - BETA) / (MICROS * ROWS * REPLICAS)

bf16 = jnp.bfloat16
f32 = jnp.float32

VM = pl.BlockSpec(memory_space=pltpu.VMEM)
ANY = pl.BlockSpec(memory_space=pl.ANY)
DMA = pltpu.SemaphoreType.DMA


SIDE = [micro % 2 for micro in range(MICROS)]
ORDER = [[m for m in range(MICROS) if SIDE[m] == side] for side in range(2)]


def at_work(tick, stage_of):
    found = {s: tick - stage_of(s // 2) for s in range(SECTIONS)}
    return {s: number for s, number in found.items() if 0 <= number < 2}


def home_source(section, micro):
    stage, side = section // 2, section % 2
    tick = stage + ORDER[SIDE[micro]].index(micro)
    if SIDE[micro] != side:
        return ("ex", tick)
    if side == 1:
        return ("mid", tick)
    return ("arr", tick) if stage else ("in", micro)


def call(kernel, out_shape, in_specs, out_specs, scratch, name, mib, flops=0, moved=0, after=0):
    def whole(*refs):
        kernel(*refs[: len(in_specs)], *refs[len(in_specs) + after :])

    return pl.pallas_call(
        whole,
        out_shape=out_shape,
        in_specs=in_specs + [ANY] * after,
        out_specs=out_specs,
        scratch_shapes=scratch,
        compiler_params=pltpu.CompilerParams(vmem_limit_bytes=mib << 20),
        cost_estimate=pl.CostEstimate(flops=flops, bytes_accessed=moved, transcendentals=0),
        name=name,
    )


def rows_of(rows=ROWS, cols=W, kind=bf16):
    return jax.ShapeDtypeStruct((rows, cols), kind)


LAYER_COST = dict(flops=2 * ROWS * W * W, moved=W * W * 2)
PAIR_COST = dict(flops=4 * ROWS * W * W, moved=W * W * 4)


def is_any(value, numbers):
    return functools.reduce(jnp.logical_or, [value == number for number in numbers])


def pick(section, wanted, choices, dst, sem):
    for tag, src in choices.items():
        users = [number for number, name in wanted.items() if name == tag]
        if users:

            @pl.when(is_any(section, users))
            def _():
                pltpu.make_async_copy(src, dst, sem).start()


def place():
    replica = lax.axis_index("dp")
    return replica // 8, lax.rem(replica // 2, RING), lax.rem(replica, 2)


def each_block(body):
    @pl.loop(0, NBLK // 4)
    def _(group):
        for k in range(4):
            body(pl.ds(pl.multiple_of((group * 4 + k) * BLK, BLK), BLK))


def forward_layer(x_ref, w_ref, h_ref, slope_ref):
    def body(cols):
        squashed = jnp.tanh(jnp.dot(x_ref[...], w_ref[:, cols], preferred_element_type=f32))
        h_ref[:, cols] = (x_ref[:, cols].astype(f32) + squashed).astype(bf16)
        slope_ref[:, cols] = (1.0 - squashed * squashed).astype(bf16)

    each_block(body)


def resident(array, after):
    def kernel(array_ref, out_ref, sem):
        copy = pltpu.make_async_copy(array_ref, out_ref, sem)
        copy.start()
        copy.wait()

    out = pltpu.VMEM(array.shape, array.dtype)
    return call(kernel, out, [ANY], VM, [DMA], "resident", 4, after=len(after))(in_hbm(array), *after)


def both_weights(own, other):
    def kernel(own_ref, other_ref, out_ref, sems):
        side = lax.rem(lax.axis_index("section"), 2)
        copies = [
            pltpu.make_async_copy(own_ref, out_ref.at[side], sems.at[0]),
            pltpu.make_async_copy(other_ref, out_ref.at[1 - side], sems.at[1]),
        ]
        for copy in copies:
            copy.start()
        for copy in copies:
            copy.wait()

    return call(
        kernel, pltpu.VMEM((2, W, W), bf16), [ANY] * 2, VM, [DMA((2,))], "both_weights", 4
    )(in_hbm(own), in_hbm(other))


def in_vmem(array):
    return pltpu.with_memory_space_constraint(array, pltpu.VMEM)


def in_hbm(array):
    return pltpu.with_memory_space_constraint(array, pltpu.HBM)


def forward_pair(tick, inputs, arriving, weights, after):
    working = at_work(tick, lambda stage: stage)
    first = {s: ORDER[s % 2][number] for s, number in working.items() if s < 2}

    def kernel(inputs_ref, arriving_ref, w_ref, *rest):
        h_ref, mid_ref, send_ref, even_ref, odd_ref, x_scr, sem = rest
        section = lax.axis_index("section")
        side = lax.rem(section, 2)

        @pl.when(is_any(section, working))
        def _():
            if first:

                @pl.when(is_any(section, first))
                def _():
                    pick(section, first, {m: inputs_ref.at[m] for m in range(MICROS)}, x_scr, sem)
                    pltpu.make_async_copy(inputs_ref.at[0], x_scr, sem).wait()

            if len(first) < len(working):

                @pl.when(section > 1)
                def _():
                    x_scr[...] = arriving_ref[...]

            forward_layer(x_scr, w_ref.at[0], mid_ref, even_ref)
            forward_layer(mid_ref, w_ref.at[1], h_ref, odd_ref)

            @pl.when(side == 0)
            def _():
                send_ref[...] = mid_ref[...]

            @pl.when(side == 1)
            def _():
                send_ref[...] = x_scr[...]

    return call(
        kernel,
        [rows_of()] * 5,
        [ANY, VM, VM],
        [VM] * 5,
        [pltpu.VMEM((ROWS, W), bf16), DMA],
        "forward_pair",
        12,
        after=len(after),
        **PAIR_COST,
    )(inputs, arriving, in_vmem(weights), *after)


def backward_layer(u_ref, slope_ref, w_ref, scaled, g_ref):
    scaled[...] = (u_ref[...].astype(f32) * slope_ref[...].astype(f32)).astype(bf16)

    def body(cols):
        back = lax.dot_general(
            scaled[...], w_ref[cols, :], (((1,), (1,)), ((), ())), preferred_element_type=f32
        )
        g_ref[:, cols] = (u_ref[:, cols].astype(f32) + back).astype(bf16)

    each_block(body)


def backward_pair(tick, cotangent, arriving, slopes, weights, after):
    working = at_work(tick, lambda stage: STAGES - 1 - stage)
    even_tags = {s: ("even", s // 2 + number) for s, number in working.items()}
    odd_tags = {s: ("odd", s // 2 + number) for s, number in working.items()}
    first = {s: ORDER[s % 2][number] for s, number in working.items() if s // 2 == STAGES - 1}
    names = sorted({*even_tags.values(), *odd_tags.values()})
    count = len(names)

    def kernel(cot_ref, arriving_ref, w_ref, *rest):
        choices = dict(zip(names, rest[:count]))
        low_ref, keep_ref, send_ref, u_scr, even_scr, odd_scr, scaled, sems = rest[count:]
        section = lax.axis_index("section")
        side = lax.rem(section, 2)

        @pl.when(is_any(section, working))
        def _():
            pick(section, odd_tags, choices, odd_scr, sems.at[0])
            pick(section, even_tags, choices, even_scr, sems.at[1])

            if first:
                pick(section, first, {m: cot_ref.at[m] for m in range(MICROS)}, u_scr, sems.at[2])

                @pl.when(is_any(section, first))
                def _():
                    pltpu.make_async_copy(cot_ref.at[0], u_scr, sems.at[2]).wait()

            if len(first) < len(working):

                @pl.when(jnp.logical_not(is_any(section, list(first) or [-1])))
                def _():
                    u_scr[...] = arriving_ref[...]

            pltpu.make_async_copy(rest[0], odd_scr, sems.at[0]).wait()
            pltpu.make_async_copy(rest[0], even_scr, sems.at[1]).wait()

            backward_layer(u_scr, odd_scr, w_ref.at[1], scaled, keep_ref)
            backward_layer(keep_ref, even_scr, w_ref.at[0], scaled, low_ref)

            @pl.when(side == 0)
            def _():
                send_ref[...] = keep_ref[...]
                keep_ref[...] = low_ref[...]

            @pl.when(side == 1)
            def _():
                send_ref[...] = low_ref[...]

    return call(
        kernel,
        [rows_of()] * 3,
        [ANY, VM, VM] + [ANY] * count,
        [VM] * 3,
        [pltpu.VMEM((ROWS, W), bf16)] * 4 + [DMA((3,))],
        "backward_pair",
        12,
        after=len(after),
        **PAIR_COST,
    )(cotangent, arriving, in_vmem(weights), *[slopes[name] for name in names], *after)


def collect(keeps, received, after):
    ticks = len(keeps)

    def kernel(*refs):
        choices = {("keep", b): refs[b] for b in range(ticks)}
        choices.update({("got", b): refs[ticks + b] for b in range(ticks)})
        out_ref, sems = refs[2 * ticks :]
        section = lax.axis_index("section")
        for m in range(MICROS):
            wanted = {}
            for s in range(SECTIONS):
                b = STAGES - 1 - s // 2 + ORDER[SIDE[m]].index(m)
                wanted[s] = ("keep" if SIDE[m] == s % 2 else "got", b)
            pick(section, wanted, choices, out_ref.at[m], sems.at[m])
        for m in range(MICROS):
            pltpu.make_async_copy(refs[0], out_ref.at[m], sems.at[m]).wait()

    return call(
        kernel,
        jax.ShapeDtypeStruct((MICROS, ROWS, W), bf16),
        [ANY] * (2 * ticks),
        ANY,
        [DMA((MICROS,))],
        "collect",
        8,
        after=len(after),
    )(*keeps, *received, *after)


def pack_home(inputs, held, after):
    names = list(held)

    def kernel(inputs_ref, *rest):
        choices = dict(zip(names, rest))
        choices.update({("in", m): inputs_ref.at[m] for m in range(MICROS)})
        out_ref, sems = rest[len(names) :]
        section = lax.axis_index("section")

        def slot(m):
            return out_ref.at[pl.ds(m * ROWS, ROWS)]

        for m in range(MICROS):
            pick(section, {s: home_source(s, m) for s in range(SECTIONS)}, choices, slot(m), sems.at[m])
        for m in range(MICROS):
            pltpu.make_async_copy(inputs_ref.at[m], slot(m), sems.at[m]).wait()

    return call(
        kernel,
        rows_of(MICROS * ROWS),
        [ANY] * (1 + len(names)),
        VM,
        [DMA((MICROS,))],
        "pack_home",
        8,
        after=len(after),
    )(inputs, *held.values(), *after)


def gram(own, mate):
    def kernel(own_ref, mate_ref, far_up, far_down, up, down, here, hid):
        z, x, core = place()
        tokens = MICROS * ROWS
        for number, ref in enumerate((own_ref, mate_ref)):
            span = slice(number * tokens, (number + 1) * tokens)
            hid[span, :W] = ref[...]
            hid[span, W:] = ref[:, : KW - BLK]
        jobs = [(far_up, 2, 0, 0), (far_up, 2, 1, 1), (far_down, 2, 2, 0), (far_down, 2, 3, 1)]
        jobs += [(ref, ahead, k, k) for ref, ahead in ((up, 1), (down, 3), (here, 0)) for k in range(RING)]
        for out_ref, ahead, chunk, row in jobs:
            column = lax.rem(x + ahead, RING)
            left = pl.ds(pl.multiple_of(chunk * RING * CHIP + column * CHIP, CHIP), CHIP)
            block = chunk * 2 + column // 2
            right = pl.ds(pl.multiple_of(block * BLK + core * HALF, 128), HALF)
            part = lax.dot_general(
                hid[:, left], hid[:, right], (((0,), (0,)), ((), ())), preferred_element_type=f32
            )
            out_ref[row * CHIP : (row + 1) * CHIP, :] = part.astype(bf16)

    return call(
        kernel,
        [rows_of(2 * CHIP, HALF)] * 2 + [rows_of(RING * CHIP, HALF)] * 3,
        [VM] * 2,
        [VM] * 5,
        [pltpu.VMEM((2 * MICROS * ROWS, W + KW - BLK), bf16)],
        "gram",
        32,
        flops=4 * MICROS * ROWS * W * HALF,
        moved=W * KW,
    )(own, mate)


def add_far(up, down, got_up, got_down, after):
    def kernel(up_ref, down_ref, gu_ref, gd_ref, new_up, new_down):
        near, far = slice(0, 2 * CHIP), slice(2 * CHIP, 4 * CHIP)
        new_up[near] = (up_ref[near].astype(f32) + gu_ref[...].astype(f32)).astype(bf16)
        new_up[far] = up_ref[far]
        new_down[near] = down_ref[near]
        new_down[far] = (down_ref[far].astype(f32) + gd_ref[...].astype(f32)).astype(bf16)

    return call(
        kernel,
        [rows_of(RING * CHIP, HALF)] * 2,
        [VM] * 4,
        [VM] * 2,
        [],
        "add_far",
        16,
        after=len(after),
    )(up, down, got_up, got_down, *after)


def add_near(here, got_up, got_down, after):
    def kernel(here_ref, gu_ref, gd_ref, own, one, two, three):
        z, x, core = place()
        for out_ref, mate in zip((own, one, two, three), (z, z ^ 1, z ^ 2, z ^ 3)):
            span = pl.ds(pl.multiple_of(mate * CHIP, CHIP), CHIP)
            total = here_ref[span].astype(f32) + gu_ref[span].astype(f32) + gd_ref[span].astype(f32)
            out_ref[...] = total.astype(out_ref.dtype)

    return call(
        kernel,
        [rows_of(CHIP, HALF, f32)] + [rows_of(CHIP, HALF)] * 3,
        [VM] * 3,
        [VM] * 4,
        [],
        "add_near",
        16,
        after=len(after),
    )(here, got_up, got_down, *after)


def damp(own, got, factor_old, factor_mate, after):
    def kernel(own_ref, g1, g2, g3, f_ref, fm_ref, damped_ref, sum_ref, old):
        z, x, core = place()
        block = z * 2 + x // 2
        pieces = HALF // 128
        for number in range(pieces):
            first = lax.rem(block * 2 + core * pieces + number, W // 128)
            cols = pl.ds(pl.multiple_of(first * 128, 128), 128)
            to = slice(number * 128, (number + 1) * 128)
            old[pl.ds(pl.multiple_of(core * ROWS, ROWS), ROWS), to] = f_ref[:, cols]
            old[pl.ds(pl.multiple_of((1 - core) * ROWS, ROWS), ROWS), to] = fm_ref[:, cols]
        total = own_ref[...] + g1[...].astype(f32) + g2[...].astype(f32) + g3[...].astype(f32)
        sum_ref[...] = total.astype(bf16)
        row = lax.broadcasted_iota(jnp.int32, (CHIP, HALF), 0) + lax.rem(x, 2) * CHIP
        column = lax.broadcasted_iota(jnp.int32, (CHIP, HALF), 1) + core * HALF
        diagonal = DAMPING * (row == column).astype(f32)
        damped_ref[...] = (BETA * old[...] + SCALE * total + diagonal).astype(bf16)

    return call(
        kernel,
        [rows_of(CHIP, HALF)] * 2,
        [VM] * 6,
        [VM] * 2,
        [pltpu.VMEM((CHIP, HALF), f32)],
        "damp",
        16,
        after=len(after),
    )(own, *got, factor_old, factor_mate, *after)


def stack_chunks(own, got, after):
    def kernel(own_ref, g1, g2, g3, out_ref):
        z, x, core = place()
        for ref, mate in zip((own_ref, g1, g2, g3), (z, z ^ 1, z ^ 2, z ^ 3)):
            out_ref[pl.ds(pl.multiple_of(mate * CHIP, CHIP), CHIP)] = ref[...]

    return call(
        kernel, rows_of(RING * CHIP, HALF), [VM] * 4, VM, [], "stack_chunks", 16, after=len(after)
    )(own, *got, *after)


def block_cols(number):
    return pl.ds(pl.multiple_of(number * BLK, BLK), BLK)


def kept_columns(stale_rows, after):
    def kernel(s_ref, out_ref):
        block = lax.axis_index("dp") // (BLK // ROWS)
        for k in range(KEEP):
            out_ref[:, k * BLK : (k + 1) * BLK] = s_ref[:, block_cols(lax.rem(block + k, NBLK))]

    return call(
        kernel, rows_of(cols=KW), [VM], VM, [], "kept_columns", 8, after=len(after)
    )(stale_rows, *after)


def times_symmetric(left_ref, mat_ref, j):
    total = None
    for i in range(NBLK):
        left = left_ref[:, i * BLK : (i + 1) * BLK]
        k = (j - i) % NBLK
        if k < KEEP:
            block = mat_ref[i * BLK : (i + 1) * BLK, k * BLK : (k + 1) * BLK]
            part = jnp.dot(left, block, preferred_element_type=f32)
        else:
            k = (i - j) % NBLK
            block = mat_ref[j * BLK : (j + 1) * BLK, k * BLK : (k + 1) * BLK]
            part = lax.dot_general(left, block, (((1,), (1,)), ((), ())), preferred_element_type=f32)
        total = part if total is None else total + part
    return total


def refresh(pieces, mate_pieces, stale_all, stale_rows, sums, mate_sums, factor_old, after):
    def kernel(sa_ref, s_ref, g_ref, gm_ref, f_ref, *rest):
        count = len(pieces)
        refs = rest[: 2 * count]
        factor_ref, inv_ref, damped, mid, turn, sums_scr, sems = rest[2 * count :]
        z, x, core = place()
        copies = []
        for whose in range(2):
            side = core if whose == 0 else 1 - core
            cols = pl.ds(pl.multiple_of(side * HALF, 128), HALF)
            for number, (_, ahead, first, chunks) in enumerate(pieces):
                ref = refs[whose * count + number]
                column = lax.rem(x + ahead, RING)
                for k in range(chunks):
                    start = (first + k) * RING * CHIP + column * CHIP
                    to = damped.at[pl.ds(pl.multiple_of(start, CHIP), CHIP), cols]
                    source = ref.at[pl.ds(k * CHIP, CHIP)]
                    copy = pltpu.make_async_copy(source, to, sems.at[len(copies)])
                    copy.start()
                    copies.append(copy)
        sums_scr[:, pl.ds(pl.multiple_of(core * HALF, 128), HALF)] = g_ref[...].astype(f32)
        sums_scr[:, pl.ds(pl.multiple_of((1 - core) * HALF, 128), HALF)] = gm_ref[...].astype(f32)
        block = z * 2 + x // 2
        own = pl.ds(pl.multiple_of(core * ROWS, ROWS), ROWS)
        for k in range(KEEP):
            cols = block_cols(lax.rem(block + k, NBLK))
            factor_ref[:, cols] = BETA * f_ref[:, cols] + SCALE * sums_scr[own, k * BLK : (k + 1) * BLK]
        for copy in copies:
            copy.wait()
        for j in range(NBLK):
            mid[:, j * BLK : (j + 1) * BLK] = times_symmetric(s_ref, damped, j).astype(bf16)
        for j in range(NBLK):
            cols = slice(j * BLK, (j + 1) * BLK)
            inv_ref[:, cols] = (2.0 * s_ref[:, cols].astype(f32) - times_symmetric(mid, sa_ref, j)).astype(bf16)
        for k in range(1, NBLK - KEEP + 1):
            other = lax.rem(block + NBLK - k, NBLK)
            lanes = pl.ds(pl.multiple_of(k * BLK + lax.rem(x, 2) * CHIP, CHIP), CHIP)
            turn[...] = damped[block_cols(other), lanes].astype(f32).T
            factor_ref[:, block_cols(other)] = turn[own, :]

    arrays = [piece[0] for piece in pieces]
    total = 2 * sum(piece[3] for piece in pieces)
    return call(
        kernel,
        [rows_of(kind=f32), rows_of()],
        [VM] * 5 + [ANY] * (2 * len(pieces)),
        [VM] * 2,
        [
            pltpu.VMEM((W, KW), bf16),
            pltpu.VMEM((ROWS, W), bf16),
            pltpu.VMEM((CHIP, BLK), f32),
            pltpu.VMEM((CHIP, KW), f32),
            DMA((total,)),
        ],
        "refresh",
        24,
        flops=4 * ROWS * W * W,
        moved=4 * W * KW,
        after=len(after),
    )(in_vmem(stale_all), in_hbm(stale_rows), sums, mate_sums, in_hbm(factor_old), *arrays, *mate_pieces, *after)


def hop(block, pairs):
    return lax.ppermute(block, "section", pairs)


def to_core(block):
    return lax.ppermute(block, "dp", [(r, r ^ 1) for r in range(REPLICAS)])


def along_x(block, step):
    return lax.ppermute(block, "dp", [(r, r // 8 * 8 + (r + 2 * step) % 8) for r in range(REPLICAS)])


def across_z(block, bits):
    return lax.ppermute(block, "dp", [(r, r ^ (8 * bits)) for r in range(REPLICAS)])


def per_device(inputs, cotangent, weight, factor_old, stale_inverse):
    factor_old = factor_old[0]
    stale_rows = stale_inverse[0]

    share = lax.dynamic_slice_in_dim(weight[0], lax.axis_index("dp") * ROWS, ROWS, 0)
    share = hop(share, [(s, s ^ 1) for s in range(SECTIONS)])
    weights = both_weights(weight[0], lax.all_gather(share, "dp", axis=0, tiled=True))
    stale_all = lax.all_gather(kept_columns(stale_rows, [share]), "dp", axis=0, tiled=True)
    factor_mate = to_core(factor_old)

    arriving = inputs[0]
    held, slopes = {}, {}
    for tick in range(TICKS):
        leaving, held["mid", tick], sending, slopes["even", tick], slopes["odd", tick] = forward_pair(
            tick, inputs, arriving, weights, [held["ex", tick - 2]] if tick >= 2 else []
        )
        working = at_work(tick, lambda stage: stage)
        held["ex", tick] = hop(sending, [(s, s ^ 1) for s in working])
        if tick < TICKS - 1:
            arriving = held["arr", tick + 1] = hop(leaving, [(s, s + 2) for s in working if s // 2 < STAGES - 1])

    state = dict(arriving=cotangent[0])
    keeps, received = [], []

    def backward(tick, *after):
        low, keep, send = backward_pair(
            tick, cotangent, state["arriving"], slopes, weights, after
        )
        working = at_work(tick, lambda stage: STAGES - 1 - stage)
        route = [(s, s - 2) for s in working if s >= 2]
        if tick < STAGES:
            state["arriving"] = hop(low, route)
        received.append(hop(send, [(s, s ^ 1) for s in working]))
        keeps.append(keep)
        return state["arriving"] if tick < STAGES else keep

    backward(0)
    backward(1)
    hidden = pack_home(inputs, held, [keeps[1]])
    far_up, far_down, up, down, here = gram(hidden, to_core(hidden))
    got_up, got_down = along_x(far_up, 1), along_x(far_down, -1)
    backward(2, here)
    up, down = add_far(up, down, got_up, got_down, [keeps[2]])
    got_up, got_down = along_x(up, 1), along_x(down, -1)
    arrived = backward(3, up)
    chunk, *sending = add_near(here, got_up, got_down, [keeps[3], received[0], received[2]])
    got = [across_z(block, bits + 1) for bits, block in enumerate(sending)]
    damped, sums = damp(chunk, got, factor_old, factor_mate, [arrived])
    got = [across_z(damped, bits) for bits in (1, 2, 3)]
    mate_sums = to_core(sums)
    backward(4, damped)
    stale_all = resident(stale_all, [damped])
    mine = stack_chunks(damped, got, [stale_all, keeps[4]])
    before, behind = along_x(mine, 1), along_x(mine, -1)
    far_low = along_x(before[: 2 * CHIP], 1)
    far_high = along_x(behind[2 * CHIP :], -1)
    pieces = [(mine, 0, 0, 4), (before, 3, 0, 4), (behind, 1, 0, 4), (far_low, 2, 0, 2), (far_high, 2, 2, 2)]
    mate_pieces = [to_core(piece[0]) for piece in pieces]
    grads = collect(keeps, received, [mine])
    factor, refined = refresh(
        pieces, mate_pieces, stale_all, stale_rows, sums, mate_sums, factor_old, [grads]
    )
    return (grads[None], factor[None], refined[None])


def solution(mesh):
    placed = (
        P(None, "dp", None),
        P(None, "dp", None),
        P("section", None, None),
        P("section", "dp", None),
        P("section", "dp", None),
    )
    return jax.shard_map(
        per_device,
        mesh=mesh,
        in_specs=placed,
        out_specs=(
            P("section", None, "dp", None),
            P("section", "dp", None),
            P("section", "dp", None),
        ),
        check_vma=False,
    )
```

```python
import functools

import jax
import jax.numpy as jnp
from jax import lax
from jax.experimental import pallas as pl
from jax.experimental.pallas import tpu as pltpu
from jax.sharding import PartitionSpec as P

BETA = 0.25
DAMPING = 1.0

SECTIONS = 8
STAGES = SECTIONS // 2
REPLICAS = 32
MICROS = 4
ROWS = 64
W = 2048
BLK = 256
NBLK = W // BLK
KEEP = NBLK // 2 + 1
KW = KEEP * BLK
HALF = KW // 2
CHIP = 2 * ROWS
RING = 4
TICKS = STAGES + 1
SCALE = (1.0 - BETA) / (MICROS * ROWS * REPLICAS)

bf16 = jnp.bfloat16
f32 = jnp.float32

VM = pl.BlockSpec(memory_space=pltpu.VMEM)
ANY = pl.BlockSpec(memory_space=pl.ANY)
DMA = pltpu.SemaphoreType.DMA


SIDE = [micro % 2 for micro in range(MICROS)]
ORDER = [[m for m in range(MICROS) if SIDE[m] == side] for side in range(2)]


def at_work(tick, stage_of):
    found = {s: tick - stage_of(s // 2) for s in range(SECTIONS)}
    return {s: number for s, number in found.items() if 0 <= number < 2}


def home_source(section, micro):
    stage, side = section // 2, section % 2
    tick = stage + ORDER[SIDE[micro]].index(micro)
    if SIDE[micro] != side:
        return ("ex", tick)
    if side == 1:
        return ("mid", tick)
    return ("arr", tick) if stage else ("in", micro)


def call(kernel, out_shape, in_specs, out_specs, scratch, name, mib, flops=0, moved=0, after=0):
    def whole(*refs):
        kernel(*refs[: len(in_specs)], *refs[len(in_specs) + after :])

    return pl.pallas_call(
        whole,
        out_shape=out_shape,
        in_specs=in_specs + [ANY] * after,
        out_specs=out_specs,
        scratch_shapes=scratch,
        compiler_params=pltpu.CompilerParams(vmem_limit_bytes=mib << 20),
        cost_estimate=pl.CostEstimate(flops=flops, bytes_accessed=moved, transcendentals=0),
        name=name,
    )


def rows_of(rows=ROWS, cols=W, kind=bf16):
    return jax.ShapeDtypeStruct((rows, cols), kind)


LAYER_COST = dict(flops=2 * ROWS * W * W, moved=W * W * 2)
PAIR_COST = dict(flops=4 * ROWS * W * W, moved=W * W * 4)


def is_any(value, numbers):
    return functools.reduce(jnp.logical_or, [value == number for number in numbers])


def pick(section, wanted, choices, dst, sem):
    for tag, src in choices.items():
        users = [number for number, name in wanted.items() if name == tag]
        if users:

            @pl.when(is_any(section, users))
            def _():
                pltpu.make_async_copy(src, dst, sem).start()


def place():
    replica = lax.axis_index("dp")
    return replica // 8, lax.rem(replica // 2, RING), lax.rem(replica, 2)


def each_block(body, together):
    @pl.loop(0, NBLK // together)
    def _(group):
        for k in range(together):
            body(pl.ds(pl.multiple_of((group * together + k) * BLK, BLK), BLK))


def forward_layer(x_ref, w_ref, h_ref, slope_ref):
    def body(cols):
        squashed = jnp.tanh(jnp.dot(x_ref[...], w_ref[:, cols], preferred_element_type=f32))
        h_ref[:, cols] = (x_ref[:, cols].astype(f32) + squashed).astype(bf16)
        slope_ref[:, cols] = (1.0 - squashed * squashed).astype(bf16)

    each_block(body, 8)


def resident(array, after):
    def kernel(array_ref, out_ref, sem):
        copy = pltpu.make_async_copy(array_ref, out_ref, sem)
        copy.start()
        copy.wait()

    out = pltpu.VMEM(array.shape, array.dtype)
    return call(kernel, out, [ANY], VM, [DMA], "resident", 4, after=len(after))(in_hbm(array), *after)


def both_weights(own, other):
    def kernel(own_ref, other_ref, out_ref, sems):
        side = lax.rem(lax.axis_index("section"), 2)
        copies = [
            pltpu.make_async_copy(own_ref, out_ref.at[side], sems.at[0]),
            pltpu.make_async_copy(other_ref, out_ref.at[1 - side], sems.at[1]),
        ]
        for copy in copies:
            copy.start()
        for copy in copies:
            copy.wait()

    return call(
        kernel, pltpu.VMEM((2, W, W), bf16), [ANY] * 2, VM, [DMA((2,))], "both_weights", 4
    )(in_hbm(own), in_hbm(other))


def in_vmem(array):
    return pltpu.with_memory_space_constraint(array, pltpu.VMEM)


def in_hbm(array):
    return pltpu.with_memory_space_constraint(array, pltpu.HBM)


def forward_pair(tick, inputs, arriving, weights, after):
    working = at_work(tick, lambda stage: stage)
    first = {s: ORDER[s % 2][number] for s, number in working.items() if s < 2}

    def kernel(inputs_ref, arriving_ref, w_ref, *rest):
        h_ref, mid_ref, send_ref, even_ref, odd_ref, x_scr, sem = rest
        section = lax.axis_index("section")
        side = lax.rem(section, 2)

        @pl.when(is_any(section, working))
        def _():
            if first:

                @pl.when(is_any(section, first))
                def _():
                    pick(section, first, {m: inputs_ref.at[m] for m in range(MICROS)}, x_scr, sem)
                    pltpu.make_async_copy(inputs_ref.at[0], x_scr, sem).wait()

            if len(first) < len(working):

                @pl.when(section > 1)
                def _():
                    x_scr[...] = arriving_ref[...]

            forward_layer(x_scr, w_ref.at[0], mid_ref, even_ref)
            forward_layer(mid_ref, w_ref.at[1], h_ref, odd_ref)

            @pl.when(side == 0)
            def _():
                send_ref[...] = mid_ref[...]

            @pl.when(side == 1)
            def _():
                send_ref[...] = x_scr[...]

    return call(
        kernel,
        [rows_of()] * 5,
        [ANY, VM, VM],
        [VM] * 5,
        [pltpu.VMEM((ROWS, W), bf16), DMA],
        "forward_pair",
        12,
        after=len(after),
        **PAIR_COST,
    )(inputs, arriving, in_vmem(weights), *after)


def backward_layer(u_ref, slope_ref, w_ref, scaled, g_ref):
    scaled[...] = (u_ref[...].astype(f32) * slope_ref[...].astype(f32)).astype(bf16)

    def body(cols):
        back = lax.dot_general(
            scaled[...], w_ref[cols, :], (((1,), (1,)), ((), ())), preferred_element_type=f32
        )
        g_ref[:, cols] = (u_ref[:, cols].astype(f32) + back).astype(bf16)

    each_block(body, 4)


def backward_pair(tick, cotangent, arriving, slopes, weights, after):
    working = at_work(tick, lambda stage: STAGES - 1 - stage)
    even_tags = {s: ("even", s // 2 + number) for s, number in working.items()}
    odd_tags = {s: ("odd", s // 2 + number) for s, number in working.items()}
    first = {s: ORDER[s % 2][number] for s, number in working.items() if s // 2 == STAGES - 1}
    names = sorted({*even_tags.values(), *odd_tags.values()})
    count = len(names)

    def kernel(cot_ref, arriving_ref, w_ref, *rest):
        choices = dict(zip(names, rest[:count]))
        low_ref, keep_ref, send_ref, u_scr, even_scr, odd_scr, scaled, sems = rest[count:]
        section = lax.axis_index("section")
        side = lax.rem(section, 2)

        @pl.when(is_any(section, working))
        def _():
            pick(section, odd_tags, choices, odd_scr, sems.at[0])
            pick(section, even_tags, choices, even_scr, sems.at[1])

            if first:
                pick(section, first, {m: cot_ref.at[m] for m in range(MICROS)}, u_scr, sems.at[2])

                @pl.when(is_any(section, first))
                def _():
                    pltpu.make_async_copy(cot_ref.at[0], u_scr, sems.at[2]).wait()

            if len(first) < len(working):

                @pl.when(jnp.logical_not(is_any(section, list(first) or [-1])))
                def _():
                    u_scr[...] = arriving_ref[...]

            pltpu.make_async_copy(rest[0], odd_scr, sems.at[0]).wait()
            pltpu.make_async_copy(rest[0], even_scr, sems.at[1]).wait()

            backward_layer(u_scr, odd_scr, w_ref.at[1], scaled, keep_ref)
            backward_layer(keep_ref, even_scr, w_ref.at[0], scaled, low_ref)

            @pl.when(side == 0)
            def _():
                send_ref[...] = keep_ref[...]
                keep_ref[...] = low_ref[...]

            @pl.when(side == 1)
            def _():
                send_ref[...] = low_ref[...]

    return call(
        kernel,
        [rows_of()] * 3,
        [ANY, VM, VM] + [ANY] * count,
        [VM] * 3,
        [pltpu.VMEM((ROWS, W), bf16)] * 4 + [DMA((3,))],
        "backward_pair",
        12,
        after=len(after),
        **PAIR_COST,
    )(cotangent, arriving, in_vmem(weights), *[slopes[name] for name in names], *after)


def collect(keeps, received, after):
    ticks = len(keeps)

    def kernel(*refs):
        choices = {("keep", b): refs[b] for b in range(ticks)}
        choices.update({("got", b): refs[ticks + b] for b in range(ticks)})
        out_ref, sems = refs[2 * ticks :]
        section = lax.axis_index("section")
        for m in range(MICROS):
            wanted = {}
            for s in range(SECTIONS):
                b = STAGES - 1 - s // 2 + ORDER[SIDE[m]].index(m)
                wanted[s] = ("keep" if SIDE[m] == s % 2 else "got", b)
            pick(section, wanted, choices, out_ref.at[m], sems.at[m])
        for m in range(MICROS):
            pltpu.make_async_copy(refs[0], out_ref.at[m], sems.at[m]).wait()

    return call(
        kernel,
        jax.ShapeDtypeStruct((MICROS, ROWS, W), bf16),
        [ANY] * (2 * ticks),
        ANY,
        [DMA((MICROS,))],
        "collect",
        8,
        after=len(after),
    )(*keeps, *received, *after)


def pack_home(inputs, held, after):
    names = list(held)

    def kernel(inputs_ref, *rest):
        choices = dict(zip(names, rest))
        choices.update({("in", m): inputs_ref.at[m] for m in range(MICROS)})
        out_ref, sems = rest[len(names) :]
        section = lax.axis_index("section")

        def slot(m):
            return out_ref.at[pl.ds(m * ROWS, ROWS)]

        for m in range(MICROS):
            pick(section, {s: home_source(s, m) for s in range(SECTIONS)}, choices, slot(m), sems.at[m])
        for m in range(MICROS):
            pltpu.make_async_copy(inputs_ref.at[m], slot(m), sems.at[m]).wait()

    return call(
        kernel,
        rows_of(MICROS * ROWS),
        [ANY] * (1 + len(names)),
        VM,
        [DMA((MICROS,))],
        "pack_home",
        8,
        after=len(after),
    )(inputs, *held.values(), *after)


def gram(own, mate):
    def kernel(own_ref, mate_ref, far_up, far_down, up, down, here, hid):
        z, x, core = place()
        tokens = MICROS * ROWS
        for number, ref in enumerate((own_ref, mate_ref)):
            span = slice(number * tokens, (number + 1) * tokens)
            hid[span, :W] = ref[...]
            hid[span, W:] = ref[:, : KW - BLK]
        jobs = [(far_up, 2, 0, 0), (far_up, 2, 1, 1), (far_down, 2, 2, 0), (far_down, 2, 3, 1)]
        jobs += [(ref, ahead, k, k) for ref, ahead in ((up, 1), (down, 3), (here, 0)) for k in range(RING)]
        for out_ref, ahead, chunk, row in jobs:
            column = lax.rem(x + ahead, RING)
            left = pl.ds(pl.multiple_of(chunk * RING * CHIP + column * CHIP, CHIP), CHIP)
            block = chunk * 2 + column // 2
            right = pl.ds(pl.multiple_of(block * BLK + core * HALF, 128), HALF)
            part = lax.dot_general(
                hid[:, left], hid[:, right], (((0,), (0,)), ((), ())), preferred_element_type=f32
            )
            out_ref[row * CHIP : (row + 1) * CHIP, :] = part.astype(bf16)

    return call(
        kernel,
        [rows_of(2 * CHIP, HALF)] * 2 + [rows_of(RING * CHIP, HALF)] * 3,
        [VM] * 2,
        [VM] * 5,
        [pltpu.VMEM((2 * MICROS * ROWS, W + KW - BLK), bf16)],
        "gram",
        32,
        flops=4 * MICROS * ROWS * W * HALF,
        moved=W * KW,
    )(own, mate)


def add_far(up, down, got_up, got_down, after):
    def kernel(up_ref, down_ref, gu_ref, gd_ref, new_up, new_down):
        near, far = slice(0, 2 * CHIP), slice(2 * CHIP, 4 * CHIP)
        new_up[near] = (up_ref[near].astype(f32) + gu_ref[...].astype(f32)).astype(bf16)
        new_up[far] = up_ref[far]
        new_down[near] = down_ref[near]
        new_down[far] = (down_ref[far].astype(f32) + gd_ref[...].astype(f32)).astype(bf16)

    return call(
        kernel,
        [rows_of(RING * CHIP, HALF)] * 2,
        [VM] * 4,
        [VM] * 2,
        [],
        "add_far",
        16,
        after=len(after),
    )(up, down, got_up, got_down, *after)


def add_near(here, got_up, got_down, after):
    def kernel(here_ref, gu_ref, gd_ref, own, one, two, three):
        z, x, core = place()
        for out_ref, mate in zip((own, one, two, three), (z, z ^ 1, z ^ 2, z ^ 3)):
            span = pl.ds(pl.multiple_of(mate * CHIP, CHIP), CHIP)
            total = here_ref[span].astype(f32) + gu_ref[span].astype(f32) + gd_ref[span].astype(f32)
            out_ref[...] = total.astype(out_ref.dtype)

    return call(
        kernel,
        [rows_of(CHIP, HALF, f32)] + [rows_of(CHIP, HALF)] * 3,
        [VM] * 3,
        [VM] * 4,
        [],
        "add_near",
        16,
        after=len(after),
    )(here, got_up, got_down, *after)


def damp(own, got, factor_old, factor_mate, after):
    def kernel(own_ref, g1, g2, g3, f_ref, fm_ref, damped_ref, sum_ref, old):
        z, x, core = place()
        block = z * 2 + x // 2
        pieces = HALF // 128
        for number in range(pieces):
            first = lax.rem(block * 2 + core * pieces + number, W // 128)
            cols = pl.ds(pl.multiple_of(first * 128, 128), 128)
            to = slice(number * 128, (number + 1) * 128)
            old[pl.ds(pl.multiple_of(core * ROWS, ROWS), ROWS), to] = f_ref[:, cols]
            old[pl.ds(pl.multiple_of((1 - core) * ROWS, ROWS), ROWS), to] = fm_ref[:, cols]
        total = own_ref[...] + g1[...].astype(f32) + g2[...].astype(f32) + g3[...].astype(f32)
        sum_ref[...] = total.astype(bf16)
        row = lax.broadcasted_iota(jnp.int32, (CHIP, HALF), 0) + lax.rem(x, 2) * CHIP
        column = lax.broadcasted_iota(jnp.int32, (CHIP, HALF), 1) + core * HALF
        diagonal = DAMPING * (row == column).astype(f32)
        damped_ref[...] = (BETA * old[...] + SCALE * total + diagonal).astype(bf16)

    return call(
        kernel,
        [rows_of(CHIP, HALF)] * 2,
        [VM] * 6,
        [VM] * 2,
        [pltpu.VMEM((CHIP, HALF), f32)],
        "damp",
        16,
        after=len(after),
    )(own, *got, factor_old, factor_mate, *after)


def stack_chunks(own, got, after):
    def kernel(own_ref, g1, g2, g3, out_ref):
        z, x, core = place()
        for ref, mate in zip((own_ref, g1, g2, g3), (z, z ^ 1, z ^ 2, z ^ 3)):
            out_ref[pl.ds(pl.multiple_of(mate * CHIP, CHIP), CHIP)] = ref[...]

    return call(
        kernel, rows_of(RING * CHIP, HALF), [VM] * 4, VM, [], "stack_chunks", 16, after=len(after)
    )(own, *got, *after)


def block_cols(number):
    return pl.ds(pl.multiple_of(number * BLK, BLK), BLK)


def kept_columns(stale_rows, after):
    def kernel(s_ref, out_ref):
        block = lax.axis_index("dp") // (BLK // ROWS)
        for k in range(KEEP):
            out_ref[:, k * BLK : (k + 1) * BLK] = s_ref[:, block_cols(lax.rem(block + k, NBLK))]

    return call(
        kernel, rows_of(cols=KW), [VM], VM, [], "kept_columns", 8, after=len(after)
    )(stale_rows, *after)


def times_symmetric(left_ref, mat_ref, j):
    total = None
    for i in range(NBLK):
        left = left_ref[:, i * BLK : (i + 1) * BLK]
        k = (j - i) % NBLK
        if k < KEEP:
            block = mat_ref[i * BLK : (i + 1) * BLK, k * BLK : (k + 1) * BLK]
            part = jnp.dot(left, block, preferred_element_type=f32)
        else:
            k = (i - j) % NBLK
            block = mat_ref[j * BLK : (j + 1) * BLK, k * BLK : (k + 1) * BLK]
            part = lax.dot_general(left, block, (((1,), (1,)), ((), ())), preferred_element_type=f32)
        total = part if total is None else total + part
    return total


def refresh(pieces, mate_pieces, stale_all, stale_rows, sums, mate_sums, factor_old, after):
    def kernel(sa_ref, s_ref, g_ref, gm_ref, f_ref, *rest):
        count = len(pieces)
        refs = rest[: 2 * count]
        factor_ref, inv_ref, damped, mid, turn, sums_scr, sems = rest[2 * count :]
        z, x, core = place()
        copies = []
        for whose in range(2):
            side = core if whose == 0 else 1 - core
            cols = pl.ds(pl.multiple_of(side * HALF, 128), HALF)
            for number, (_, ahead, first, chunks) in enumerate(pieces):
                ref = refs[whose * count + number]
                column = lax.rem(x + ahead, RING)
                for k in range(chunks):
                    start = (first + k) * RING * CHIP + column * CHIP
                    to = damped.at[pl.ds(pl.multiple_of(start, CHIP), CHIP), cols]
                    source = ref.at[pl.ds(k * CHIP, CHIP)]
                    copy = pltpu.make_async_copy(source, to, sems.at[len(copies)])
                    copy.start()
                    copies.append(copy)
        sums_scr[:, pl.ds(pl.multiple_of(core * HALF, 128), HALF)] = g_ref[...].astype(f32)
        sums_scr[:, pl.ds(pl.multiple_of((1 - core) * HALF, 128), HALF)] = gm_ref[...].astype(f32)
        block = z * 2 + x // 2
        own = pl.ds(pl.multiple_of(core * ROWS, ROWS), ROWS)
        for k in range(KEEP):
            cols = block_cols(lax.rem(block + k, NBLK))
            factor_ref[:, cols] = BETA * f_ref[:, cols] + SCALE * sums_scr[own, k * BLK : (k + 1) * BLK]
        for copy in copies:
            copy.wait()
        for j in range(NBLK):
            mid[:, j * BLK : (j + 1) * BLK] = times_symmetric(s_ref, damped, j).astype(bf16)
        for j in range(NBLK):
            cols = slice(j * BLK, (j + 1) * BLK)
            inv_ref[:, cols] = (2.0 * s_ref[:, cols].astype(f32) - times_symmetric(mid, sa_ref, j)).astype(bf16)
        for k in range(1, NBLK - KEEP + 1):
            other = lax.rem(block + NBLK - k, NBLK)
            lanes = pl.ds(pl.multiple_of(k * BLK + lax.rem(x, 2) * CHIP, CHIP), CHIP)
            turn[...] = damped[block_cols(other), lanes].astype(f32).T
            factor_ref[:, block_cols(other)] = turn[own, :]

    arrays = [piece[0] for piece in pieces]
    total = 2 * sum(piece[3] for piece in pieces)
    return call(
        kernel,
        [rows_of(kind=f32), rows_of()],
        [VM] * 5 + [ANY] * (2 * len(pieces)),
        [VM] * 2,
        [
            pltpu.VMEM((W, KW), bf16),
            pltpu.VMEM((ROWS, W), bf16),
            pltpu.VMEM((CHIP, BLK), f32),
            pltpu.VMEM((CHIP, KW), f32),
            DMA((total,)),
        ],
        "refresh",
        24,
        flops=4 * ROWS * W * W,
        moved=4 * W * KW,
        after=len(after),
    )(in_vmem(stale_all), in_hbm(stale_rows), sums, mate_sums, in_hbm(factor_old), *arrays, *mate_pieces, *after)


def hop(block, pairs):
    return lax.ppermute(block, "section", pairs)


def to_core(block):
    return lax.ppermute(block, "dp", [(r, r ^ 1) for r in range(REPLICAS)])


def along_x(block, step):
    return lax.ppermute(block, "dp", [(r, r // 8 * 8 + (r + 2 * step) % 8) for r in range(REPLICAS)])


def across_z(block, bits):
    return lax.ppermute(block, "dp", [(r, r ^ (8 * bits)) for r in range(REPLICAS)])


def per_device(inputs, cotangent, weight, factor_old, stale_inverse):
    factor_old = factor_old[0]
    stale_rows = stale_inverse[0]

    share = lax.dynamic_slice_in_dim(weight[0], lax.axis_index("dp") * ROWS, ROWS, 0)
    share = hop(share, [(s, s ^ 1) for s in range(SECTIONS)])
    weights = both_weights(weight[0], lax.all_gather(share, "dp", axis=0, tiled=True))
    stale_all = lax.all_gather(kept_columns(stale_rows, [share]), "dp", axis=0, tiled=True)
    factor_mate = to_core(factor_old)

    arriving = inputs[0]
    held, slopes = {}, {}
    for tick in range(TICKS):
        leaving, held["mid", tick], sending, slopes["even", tick], slopes["odd", tick] = forward_pair(
            tick, inputs, arriving, weights, [held["ex", tick - 2]] if tick >= 2 else []
        )
        working = at_work(tick, lambda stage: stage)
        held["ex", tick] = hop(sending, [(s, s ^ 1) for s in working])
        if tick < TICKS - 1:
            arriving = held["arr", tick + 1] = hop(leaving, [(s, s + 2) for s in working if s // 2 < STAGES - 1])

    state = dict(arriving=cotangent[0])
    keeps, received = [], []

    def backward(tick, *after):
        low, keep, send = backward_pair(
            tick, cotangent, state["arriving"], slopes, weights, after
        )
        working = at_work(tick, lambda stage: STAGES - 1 - stage)
        route = [(s, s - 2) for s in working if s >= 2]
        if tick < STAGES:
            state["arriving"] = hop(low, route)
        received.append(hop(send, [(s, s ^ 1) for s in working]))
        keeps.append(keep)
        return state["arriving"] if tick < STAGES else keep

    backward(0)
    backward(1)
    hidden = pack_home(inputs, held, [keeps[1]])
    far_up, far_down, up, down, here = gram(hidden, to_core(hidden))
    got_up, got_down = along_x(far_up, 1), along_x(far_down, -1)
    backward(2, here)
    up, down = add_far(up, down, got_up, got_down, [keeps[2]])
    got_up, got_down = along_x(up, 1), along_x(down, -1)
    arrived = backward(3, up)
    chunk, *sending = add_near(here, got_up, got_down, [keeps[3], received[0], received[2]])
    got = [across_z(block, bits + 1) for bits, block in enumerate(sending)]
    damped, sums = damp(chunk, got, factor_old, factor_mate, [arrived])
    got = [across_z(damped, bits) for bits in (1, 2, 3)]
    mate_sums = to_core(sums)
    backward(4, damped)
    stale_all = resident(stale_all, [damped])
    mine = stack_chunks(damped, got, [stale_all, keeps[4]])
    before, behind = along_x(mine, 1), along_x(mine, -1)
    far_low = along_x(before[: 2 * CHIP], 1)
    far_high = along_x(behind[2 * CHIP :], -1)
    pieces = [(mine, 0, 0, 4), (before, 3, 0, 4), (behind, 1, 0, 4), (far_low, 2, 0, 2), (far_high, 2, 2, 2)]
    mate_pieces = [to_core(piece[0]) for piece in pieces]
    grads = collect(keeps, received, [mine])
    factor, refined = refresh(
        pieces, mate_pieces, stale_all, stale_rows, sums, mate_sums, factor_old, []
    )
    return (grads[None], factor[None], refined[None])


def solution(mesh):
    placed = (
        P(None, "dp", None),
        P(None, "dp", None),
        P("section", None, None),
        P("section", "dp", None),
        P("section", "dp", None),
    )
    return jax.shard_map(
        per_device,
        mesh=mesh,
        in_specs=placed,
        out_specs=(
            P("section", None, "dp", None),
            P("section", "dp", None),
            P("section", "dp", None),
        ),
        check_vma=False,
    )
```
